32 devices in a mesh: blocks: 2 (over y), space: 4 (over z), tm: 2 (over x), span: 2 (over core).
Axes of the slice: x: 2, y: 2, z: 4, core: 2. Of those that a mesh axis runs over, the one named last changes fastest.
Arguments:
- snapshots: float32 [320, 64, 512], P(('blocks', 'tm'), 'space', 'span'), parts along dimension 0, may hold values from -6 to 6
- lagrange_weights: float32 [512, 6], P(('blocks', 'tm')), parts along dimension 0, may hold values from -3 to 3
- source_start: int32 [512], P(('blocks', 'tm')), parts along dimension 0, may hold values from 0 to 156
- band_len: int32 [512], P(('blocks', 'tm')), parts along dimension 0, may hold values from 4 to 6
- band_list: int32 [8], replicated, may hold values from 0 to 15, as said below
- row_metric: float32 [64], P('space'), may hold values from 0.5 to 2
Outputs:
- spectra: float32 [256, 2, 64, 512], P(('blocks', 'space', 'tm'), None, None, 'span'), parts along dimension 0
The draws below stay inside these ranges and needn't reach their ends.
There are 2 independent parts, one for each index of `blocks`. The reference program is written for one: setup_inputs(seed, part) draws one part's arguments, and reference() takes and returns one part's arrays. A program takes and returns all parts, laid end to end along the dimension named above; an argument that names none is the same for every part. Nothing has to cross between parts.
Inputs may be any that keep to these rules, and one draw needn't show every extreme that they name: `band_list`: 8 distinct band numbers.
All inputs are finite; a program needn't handle non-finite values.
Results may differ from the reference program's by a relative error of at most 0.0001.
Values sent between devices are 32-bit elements; how exact they have to be, the bound alone decides.
A program may use at most 64 MiB of HBM per device.

```python
import math
import jax
import jax.numpy as jnp
from jax import lax

NS_DEV = 80
HALO = 16
NT = 256
BW = 8
NBANDS = 16
NL = 8
ROWS = 64
Z = 512
NS = 160
TT_DEV = 128
NFL = 64
N_TM = 2


def band_plan(key):
    folded = jax.random.fold_in(key, 11)
    key_len, key_pos = jax.random.split(folded)
    sample_ids = jnp.arange(NT)
    band_lens = jax.random.randint(key_len, (NT,), 4, 7)
    band_lens = jnp.where(sample_ids % TT_DEV == TT_DEV - 1, 4, band_lens)
    band_lens = jnp.where(sample_ids % TT_DEV == 1, 6, band_lens)
    owner_grp = sample_ids // TT_DEV
    reach_low = jnp.maximum(owner_grp * NS_DEV - HALO, 0)
    reach_high = jnp.minimum((owner_grp + 1) * NS_DEV + HALO, NS)
    pos_range = reach_high - band_lens - reach_low + 1
    random_pos = jax.random.randint(key_pos, (NT,), 0, 1048576)
    band_start = reach_low + random_pos % pos_range
    band_start = jnp.where(sample_ids % TT_DEV == 0, reach_low, band_start)
    band_start = jnp.where(sample_ids % TT_DEV == TT_DEV - 1, reach_high - band_lens, band_start)
    return (band_start.astype(jnp.int32), band_lens.astype(jnp.int32))


def draw_source_start(key, part):
    return band_plan(key)[0]


def draw_band_len(key, part):
    return band_plan(key)[1]


def draw_band_list(key, part):
    folded = jax.random.fold_in(key, 23)
    key_one, key_two = jax.random.split(folded)
    others = jax.random.permutation(key_one, NBANDS - 1)[:NL - 1]
    chosen = jnp.concatenate([others, jnp.array([NBANDS - 1])])
    return jax.random.permutation(key_two, chosen).astype(jnp.int32)


def block_scale(rng, extent, cuts, smallest, high):
    loudness, own = 1.0, jax.random.fold_in(rng, 6)
    for position, blocks in cuts:
        heights = jnp.exp(jax.random.uniform(jax.random.fold_in(own, position), (blocks,), jnp.float32, smallest / len(cuts), high / len(cuts)))
        loudness = loudness * jnp.repeat(heights, extent[position] // blocks).reshape([-1 if axis == position else 1 for axis in range(len(extent))])
    return loudness


def bell_draw(rng, dims, scale, reach, shards=(), held_as=jnp.bfloat16):
    drawn = jax.random.normal(rng, dims, jnp.float32) * scale
    if len(shards) > 0:
        drawn = block_scale(rng, dims, shards, -0.22, 0.18) * drawn
    return jnp.clip(drawn, min=-reach, max=reach).astype(held_as)


def setup_inputs(seed: int = 0, part: int = 0) -> dict:
    arg_keys = jax.random.split(jax.random.key(seed), 7)
    own_keys = jax.random.split(jax.random.fold_in(arg_keys[6], part), 7)
    snapshots = bell_draw(own_keys[0], (NS, ROWS, Z), 1.0, 6.0, ((0, 2), (1, 4), (2, 2)), jnp.float32)
    lagrange_weights = bell_draw(own_keys[1], (NT, 6), 0.5, 3.0, ((0, 2),), jnp.float32)
    source_start = draw_source_start(jax.random.fold_in(jax.random.fold_in(arg_keys[6], part), 71), part)
    band_len = draw_band_len(jax.random.fold_in(jax.random.fold_in(arg_keys[6], part), 71), part)
    band_list = draw_band_list(jax.random.fold_in(arg_keys[6], 71), part)
    row_metric = jnp.clip(jnp.exp(math.log(2.0) - 1.3862944 * jax.random.uniform(arg_keys[5], (ROWS,), jnp.float32) ** block_scale(arg_keys[5], (ROWS,), ((0, 4),), -0.2, 0.2)), 0.5, 2.0)
    return {"snapshots": snapshots, "lagrange_weights": lagrange_weights, "source_start": source_start, "band_len": band_len, "band_list": band_list, "row_metric": row_metric}


def dft_rows(band_list, row_ids, first_sample, count):
    listed_idx = row_ids // 2
    is_imag = row_ids % 2
    band_pos = listed_idx // BW
    matches = band_pos[:, None] == jnp.arange(band_list.shape[0])[None, :]
    band_of = lax.optimization_barrier(jnp.sum(jnp.where(matches, band_list[None, :], 0), axis=1))
    frequency = band_of * BW + listed_idx % BW
    sample_ids = first_sample + jnp.arange(count)
    phase_idx = frequency[:, None] * sample_ids[None, :] % NT
    angles = 2.0 * math.pi / NT * phase_idx.astype(jnp.float32)
    window = 0.5 - 0.5 * jnp.cos(2.0 * math.pi / NT * sample_ids.astype(jnp.float32))
    weighting = window / math.sqrt(NT)
    waves = jnp.where(is_imag[:, None] == 0, jnp.cos(angles), -jnp.sin(angles))
    return waves * weighting[None, :]

def reference(snapshots, lagrange_weights, source_start, band_len, band_list, row_metric):
    slot_ids = jnp.arange(6)
    columns = source_start[:, None] + slot_ids[None, :]
    active = slot_ids[None, :] < band_len[:, None]
    selected = (columns[:, :, None] == jnp.arange(NS)[None, None, :]) & active[:, :, None]
    interp_matrix = lax.optimization_barrier(jnp.sum(jnp.where(selected, lagrange_weights[:, :, None], jnp.float32(0.0)), axis=1))
    flat = snapshots.reshape(NS, ROWS * Z)
    interpolated = jnp.dot(interp_matrix, flat, precision=lax.Precision.HIGHEST).reshape(NT, ROWS, Z)
    padded = jnp.pad(interpolated, ((0, 0), (1, 1), (0, 0)))
    along_rows = 0.5 * row_metric[None, :, None] * (padded[:, 2:, :] - padded[:, :-2, :])
    along_span = 0.5 * (jnp.roll(interpolated, -1, axis=2) - jnp.roll(interpolated, 1, axis=2))
    gradients = jnp.stack((along_rows, along_span), axis=1)
    row_ids = jnp.arange(2 * NFL)
    accumulated = jnp.zeros((2 * NFL, 2 * ROWS * Z), jnp.float32)
    for group_idx in range(N_TM):
        coeffs = dft_rows(band_list, row_ids, group_idx * TT_DEV, TT_DEV)
        block = gradients[group_idx * TT_DEV:(group_idx + 1) * TT_DEV].reshape(TT_DEV, 2 * ROWS * Z)
        partial_value = jnp.dot(coeffs, block, precision=lax.Precision.HIGHEST)
        accumulated = accumulated + partial_value
    return accumulated.reshape(2 * NFL, 2, ROWS, Z)
```

```python
import math

import jax
import jax.numpy as jnp
from jax import lax
from jax.sharding import PartitionSpec as P

HALO = 16
NT = 256
BW = 8
NL = 8


def extended(cells, sides, width, closed):
    for axis, dim in sides:
        count = lax.axis_size(axis)
        ends = count if closed else count - 1
        head = lax.slice_in_dim(cells, 0, width, axis=dim)
        tail = lax.slice_in_dim(cells, cells.shape[dim] - width, cells.shape[dim], axis=dim)
        cells = jnp.concatenate(
            [
                lax.ppermute(tail, axis, [(i, (i + 1) % count) for i in range(ends)]),
                cells,
                lax.ppermute(head, axis, [((i + 1) % count, i) for i in range(ends)]),
            ],
            axis=dim,
        )
    return cells


def dft_rows(band_list, row_ids, first_sample, count):
    listed_idx = row_ids // 2
    is_imag = row_ids % 2
    band_pos = listed_idx // BW
    matches = band_pos[:, None] == jnp.arange(band_list.shape[0])[None, :]
    band_of = jnp.sum(jnp.where(matches, band_list[None, :], 0), axis=1)
    frequency = band_of * BW + listed_idx % BW
    sample_ids = first_sample + jnp.arange(count)
    phase_idx = frequency[:, None] * sample_ids[None, :] % NT
    angles = 2.0 * math.pi / NT * phase_idx.astype(jnp.float32)
    window = 0.5 - 0.5 * jnp.cos(2.0 * math.pi / NT * sample_ids.astype(jnp.float32))
    weighting = window / math.sqrt(NT)
    waves = jnp.where(is_imag[:, None] == 0, jnp.cos(angles), -jnp.sin(angles))
    return waves * weighting[None, :]


def shards(snapshots, lagrange_weights, source_start, band_len, band_list, row_metric):
    tm_index = lax.axis_index("tm")
    n_tm, n_space = lax.axis_size("tm"), lax.axis_size("space")
    steps_dev, rows_dev, span_cells = snapshots.shape
    samples = source_start.shape[0]
    reach = extended(snapshots, (("tm", 0),), HALO, False)
    reach_len = steps_dev + 2 * HALO
    anchor = tm_index * steps_dev - HALO
    slot_ids = jnp.arange(6)
    columns = source_start[:, None] + slot_ids[None, :] - anchor
    active = slot_ids[None, :] < band_len[:, None]
    selected = (columns[:, :, None] == jnp.arange(reach_len)[None, None, :]) & active[:, :, None]
    interp_matrix = jnp.sum(
        jnp.where(selected, lagrange_weights[:, :, None], jnp.float32(0.0)), axis=1
    )
    total_rows = 2 * NL * BW
    own = total_rows // (n_tm * n_space)
    positions = jnp.arange(total_rows).reshape(n_space, n_tm, own).transpose(1, 0, 2).reshape(-1)
    coeffs = dft_rows(band_list, positions, tm_index * samples, samples)
    combined = jnp.dot(coeffs, interp_matrix, precision=lax.Precision.HIGHEST)
    partial = jnp.dot(
        combined,
        reach.reshape(reach_len, rows_dev * span_cells),
        precision=lax.Precision.HIGHEST,
    )
    summed = lax.psum_scatter(partial, "tm", scatter_dimension=0, tiled=True)
    summed = summed.reshape(n_space * own, rows_dev, span_cells)
    fields = lax.all_to_all(summed, "space", split_axis=0, concat_axis=1, tiled=True)
    metric = lax.all_gather(row_metric, "space", tiled=True)
    row_padded = jnp.pad(fields, ((0, 0), (1, 1), (0, 0)))
    along_rows = 0.5 * metric[None, :, None] * (row_padded[:, 2:, :] - row_padded[:, :-2, :])
    span_padded = extended(fields, (("span", 2),), 1, True)
    along_span = 0.5 * (span_padded[:, :, 2:] - span_padded[:, :, :-2])
    return jnp.stack((along_rows, along_span), axis=1)


def solution(mesh):
    placed = (
        P(("blocks", "tm"), "space", "span"),
        P(("blocks", "tm"), None),
        P(("blocks", "tm")),
        P(("blocks", "tm")),
        P(),
        P("space"),
    )
    return jax.shard_map(
        shards,
        mesh=mesh,
        in_specs=placed,
        out_specs=P(("blocks", "space", "tm"), None, None, "span"),
        check_vma=False,
    )
```

```python
import functools
import math

import jax
import jax.numpy as jnp
from jax import lax
from jax.experimental import pallas as pl
from jax.experimental.pallas import tpu as pltpu
from jax.sharding import PartitionSpec as P

NT = 256
BW = 8
NL = 8
SLOTS = 6
LANES = 128
PAD = 8
CHUNKS = 4
MESH = pl.DeviceIdType.MESH
HIGHEST = lax.Precision.HIGHEST


def cosine(phase):
    folded = NT // 4 - jnp.minimum(phase, NT - phase)
    u = folded.astype(jnp.float32) * (2.0 * math.pi / NT)
    square = u * u
    total = jnp.full_like(u, 1.0 / math.factorial(13))
    for order in (11, 9, 7, 5, 3, 1):
        sign = 1.0 if order % 4 == 1 else -1.0
        total = total * square + sign / math.factorial(order)
    return total * u


def kernel(
    dims,
    x_ref,
    w_ref,
    start_ref,
    len_ref,
    band_ref,
    metric_ref,
    out_ref,
    packed,
    metrics,
    mixing,
    fields,
    arrived,
    final,
    edges,
    pk_send,
    pk_recv,
    mt_send,
    mt_recv,
    x_send,
    x_recv,
    z_send,
    z_recv,
    e_send,
    e_recv,
):
    n_tm, n_space, steps, rows, cells, samples, own, chunks = dims
    per = own // chunks
    total = 2 * NL * BW
    tm, space, span = lax.axis_index("tm"), lax.axis_index("space"), lax.axis_index("span")
    group = n_space * per
    tiles = cells // LANES
    pitch = tiles * rows
    flat = fields.reshape(total * pitch, LANES)

    def peer_tm(d):
        return {"tm": lax.rem(tm + d, n_tm)}

    def peer_space(d):
        return {"space": lax.rem(space + d, n_space)}

    other = {"span": 1 - span}

    barrier = pltpu.get_barrier_semaphore()
    for d in range(1, n_tm):
        pl.semaphore_signal(barrier, inc=1, device_id=peer_tm(d), device_id_type=MESH)
    for d in range(1, n_space):
        pl.semaphore_signal(barrier, inc=1, device_id=peer_space(d), device_id_type=MESH)
    pl.semaphore_signal(barrier, inc=1, device_id=other, device_id_type=MESH)

    packed[tm] = jnp.zeros((8, LANES), jnp.float32)
    packed[tm, 0:SLOTS, 0:samples] = w_ref[...]
    packed[tm, 6:7, 0:samples] = start_ref[...].astype(jnp.float32)
    packed[tm, 7:8, 0:samples] = len_ref[...].astype(jnp.float32)
    square = (rows, rows)
    diagonal = lax.broadcasted_iota(jnp.int32, square, 0) == lax.broadcasted_iota(
        jnp.int32, square, 1
    )
    column = jnp.sum(
        jnp.where(diagonal, jnp.broadcast_to(metric_ref[...], square), 0.0), axis=1, keepdims=True
    )
    mine = pl.ds(pl.multiple_of(space * rows, 8), rows)
    metrics[mine, :] = jnp.broadcast_to(0.5 * column, (rows, LANES))

    pl.semaphore_wait(barrier, n_tm - 1 + n_space - 1 + 1)

    started = []
    pk_copies = []
    for d in range(1, n_tm):
        copy = pltpu.make_async_remote_copy(
            packed.at[tm], packed.at[tm], pk_send.at[d - 1], pk_recv.at[d - 1],
            device_id=peer_tm(d), device_id_type=MESH,
        )
        copy.start()
        pk_copies.append(copy)
    mt_copies = []
    for d in range(1, n_space):
        copy = pltpu.make_async_remote_copy(
            metrics.at[mine, :], metrics.at[mine, :], mt_send.at[d - 1], mt_recv.at[d - 1],
            device_id=peer_space(d), device_id_type=MESH,
        )
        copy.start()
        mt_copies.append(copy)

    for g in range(own):
        for v in range(tiles):
            final[g, v, 0:PAD, :] = jnp.zeros((PAD, LANES), jnp.float32)
            final[g, v, PAD + n_space * rows :, :] = jnp.zeros((PAD, LANES), jnp.float32)

    p = lax.broadcasted_iota(jnp.int32, (total, LANES), 0)
    lane = lax.broadcasted_iota(jnp.int32, (total, LANES), 1)
    low = lax.rem(p, per)
    i = lax.rem(lax.div(p, per), n_space)
    j = lax.rem(lax.div(p, per * n_space), n_tm)
    c = lax.div(p, per * n_space * n_tm)
    g = (i * n_tm + j) * own + c * per + low
    listed = g >> 1
    band_pos = lax.div(listed, BW)
    band = jnp.zeros_like(p)
    for b in range(NL):
        band = jnp.where(band_pos == b, band_ref[b], band)
    frequency = band * BW + lax.rem(listed, BW)
    quarter = (NT // 4) * (g & 1)

    def dft(q):
        t = q * samples + lane
        phase = (frequency * t + quarter) & (NT - 1)
        window = 0.5 - 0.5 * cosine(t & (NT - 1))
        return cosine(phase) * (window / math.sqrt(NT))

    waves = [dft(lax.rem(tm + n_tm - d, n_tm)) for d in range(n_tm)]

    step = tm * steps + lax.broadcasted_iota(jnp.int32, (steps, LANES), 0)
    mixed = None
    for d in range(n_tm):
        q = lax.rem(tm + n_tm - d, n_tm)
        if d > 0:
            pk_copies[d - 1].wait_recv()
        table = packed[q]
        slot = step - table[6:7].astype(jnp.int32)
        slot = jnp.where(slot < table[7:8].astype(jnp.int32), slot, -1)
        weights = jnp.zeros((steps, LANES), jnp.float32)
        for s in range(SLOTS):
            weights = jnp.where(slot == s, table[s : s + 1], weights)
        term = lax.dot_general(
            waves[d], weights, (((1,), (1,)), ((), ())),
            precision=HIGHEST, preferred_element_type=jnp.float32,
        )
        mixed = term if mixed is None else mixed + term
    mixing[...] = mixed

    rows_per = n_tm * group
    x_copies, z_copies, e_copies = {}, {}, {}

    def start_x(c):
        left = mixing[c * rows_per : (c + 1) * rows_per, :]

        def body(r, carry):
            from_row = lax.div(r, 8) * (8 * tiles) + lax.rem(r, 8)
            right = jnp.concatenate(
                [x_ref[pl.ds(from_row + 8 * v, steps, stride=pitch), :] for v in range(tiles)], axis=1
            )
            value = jnp.dot(left, right, precision=HIGHEST, preferred_element_type=jnp.float32)
            for v in range(tiles):
                flat[pl.ds(c * rows_per * pitch + v * rows + r, rows_per, stride=pitch), :] = value[
                    :, v * LANES : (v + 1) * LANES
                ]
            return carry

        lax.fori_loop(0, rows, body, 0, unroll=4)
        x_copies[c] = []
        for d in range(1, n_tm):
            to = lax.rem(tm + d, n_tm)
            copy = pltpu.make_async_remote_copy(
                fields.at[pl.ds((c * n_tm + to) * group, group)],
                arrived.at[c, d - 1],
                x_send.at[c, d - 1], x_recv.at[c, d - 1],
                device_id=peer_tm(d), device_id_type=MESH,
            )
            copy.start()
            x_copies[c].append(copy)

    def start_z(c):
        for copy in x_copies[c]:
            copy.wait_recv()
        base = (c * n_tm + tm) * group

        def body(k, carry):
            value = fields[base + k]
            for d in range(1, n_tm):
                value = value + arrived[c, d - 1, k]
            fields[base + k] = value
            return carry

        lax.fori_loop(0, group, body, 0, unroll=min(4, group))
        z_copies[c] = []
        there = pl.ds(pl.multiple_of(PAD + space * rows, 8), rows)
        for d in range(1, n_space):
            to = lax.rem(space + d, n_space)
            copy = pltpu.make_async_remote_copy(
                fields.at[pl.ds(base + to * per, per)],
                final.at[pl.ds(c * per, per), pl.ds(0, tiles), there, :],
                z_send.at[c, d - 1], z_recv.at[c, d - 1],
                device_id=peer_space(d), device_id_type=MESH,
            )
            copy.start()
            z_copies[c].append(copy)
        for k in range(per):
            final[c * per + k, 0:tiles, there, :] = fields[base + space * per + k]

    inner = pl.ds(PAD, n_space * rows)

    def start_e(c):
        for copy in z_copies[c]:
            copy.wait_recv()
        first = lax.broadcasted_iota(jnp.int32, (n_space * rows, LANES), 1) == 0
        for k in range(per):
            g = c * per + k
            edges[g] = jnp.where(
                first, final[g, 0, inner, :], final[g, tiles - 1, inner, :]
            )
        copy = pltpu.make_async_remote_copy(
            edges.at[pl.ds(c * per, per)],
            final.at[pl.ds(c * per, per), tiles, inner, :],
            e_send.at[c], e_recv.at[c],
            device_id=other, device_id_type=MESH,
        )
        copy.start()
        e_copies[c] = copy

    def finish(c):
        e_copies[c].wait_recv()
        scale = metrics[...]
        for k in range(per):
            g = c * per + k
            for v in range(tiles):
                above = final[g, v, PAD + 1 : PAD + 1 + n_space * rows, :]
                below = final[g, v, PAD - 1 : PAD - 1 + n_space * rows, :]
                out_ref[g, 0, :, v * LANES : (v + 1) * LANES] = scale * (above - below)
            ring = jnp.concatenate([final[g, v, inner, :] for v in range(tiles + 1)], axis=1)
            after = pltpu.roll(ring, cells + LANES - 1, 1)
            before = pltpu.roll(ring, 1, 1)
            out_ref[g, 1] = 0.5 * (after - before)[:, 0:cells]

    for s in range(chunks + 3):
        if s < chunks:
            start_x(s)
        if 0 <= s - 1 < chunks:
            start_z(s - 1)
        if s == 2:
            for copy in mt_copies:
                copy.wait_recv()
        if 0 <= s - 2 < chunks:
            start_e(s - 2)
        if 0 <= s - 3 < chunks:
            finish(s - 3)

    for copy in pk_copies + mt_copies:
        copy.wait_send()
    for c in range(chunks):
        for copy in x_copies[c] + z_copies[c] + [e_copies[c]]:
            copy.wait_send()


def shards(snapshots, lagrange_weights, source_start, band_len, band_list, row_metric):
    n_tm, n_space = lax.axis_size("tm"), lax.axis_size("space")
    steps, rows, cells = snapshots.shape
    samples = source_start.shape[0]
    total = 2 * NL * BW
    own = total // (n_tm * n_space)
    chunks = math.gcd(own, CHUNKS)
    per = own // chunks
    dims = (n_tm, n_space, steps, rows, cells, samples, own, chunks)
    vmem = pl.BlockSpec(memory_space=pltpu.VMEM)
    f32 = jnp.float32
    dma = pltpu.SemaphoreType.DMA
    return pl.pallas_call(
        functools.partial(kernel, dims),
        out_shape=jax.ShapeDtypeStruct((own, 2, n_space * rows, cells), f32),
        in_specs=[vmem, vmem, vmem, vmem, pl.BlockSpec(memory_space=pltpu.SMEM), vmem],
        out_specs=vmem,
        scratch_shapes=[
            pltpu.VMEM((n_tm, 8, LANES), f32),
            pltpu.VMEM((n_space * rows, LANES), f32),
            pltpu.VMEM((total, steps), f32),
            pltpu.VMEM((total, cells // LANES, rows, LANES), f32),
            pltpu.VMEM((chunks, n_tm - 1, n_space * per, cells // LANES, rows, LANES), f32),
            pltpu.VMEM((own, cells // LANES + 1, n_space * rows + 2 * PAD, LANES), f32),
            pltpu.VMEM((own, n_space * rows, LANES), f32),
            dma((n_tm - 1,)),
            dma((n_tm - 1,)),
            dma((n_space - 1,)),
            dma((n_space - 1,)),
            dma((chunks, n_tm - 1)),
            dma((chunks, n_tm - 1)),
            dma((chunks, n_space - 1)),
            dma((chunks, n_space - 1)),
            dma((chunks,)),
            dma((chunks,)),
        ],
        compiler_params=pltpu.CompilerParams(
            collective_id=0, has_side_effects=True, vmem_limit_bytes=32 * 1024 * 1024
        ),
    )(
        snapshots.reshape(steps, rows // 8, 8, cells // LANES, LANES)
        .swapaxes(2, 3)
        .reshape(steps * rows * (cells // LANES), LANES),
        lagrange_weights.T,
        source_start.reshape(1, samples),
        band_len.reshape(1, samples),
        band_list,
        row_metric.reshape(1, rows),
    )


def solution(mesh):
    placed = (
        P(("blocks", "tm"), "space", "span"),
        P(("blocks", "tm"), None),
        P(("blocks", "tm")),
        P(("blocks", "tm")),
        P(),
        P("space"),
    )
    return jax.shard_map(
        shards,
        mesh=mesh,
        in_specs=placed,
        out_specs=P(("blocks", "space", "tm"), None, None, "span"),
        check_vma=False,
    )
```

```python
import functools
import math

import jax
import jax.numpy as jnp
from jax import lax
from jax.experimental import pallas as pl
from jax.experimental.pallas import tpu as pltpu
from jax.sharding import PartitionSpec as P

NT = 256
BW = 8
NL = 8
SLOTS = 6
LANES = 128
PAD = 8
CHUNKS = 8
AHEAD = 3
Z_LAG = 3
E_LAG = 2
MESH = pl.DeviceIdType.MESH
HIGHEST = lax.Precision.HIGHEST


def cosine(phase):
    folded = NT // 4 - jnp.minimum(phase, NT - phase)
    u = folded.astype(jnp.float32) * (2.0 * math.pi / NT)
    square = u * u
    total = jnp.full_like(u, 1.0 / math.factorial(13))
    for order in (11, 9, 7, 5, 3, 1):
        sign = 1.0 if order % 4 == 1 else -1.0
        total = total * square + sign / math.factorial(order)
    return total * u


def three(value):
    high = value.astype(jnp.bfloat16).astype(jnp.float32)
    rest = value - high
    middle = rest.astype(jnp.bfloat16).astype(jnp.float32)
    return high, middle, rest - middle


def kernel(
    dims,
    x_ref,
    small_ref,
    out_ref,
    parts,
    packed,
    metrics,
    mixing,
    fields,
    arrived,
    final,
    edges,
    pk_send,
    pk_recv,
    mt_send,
    mt_recv,
    x_send,
    x_recv,
    z_send,
    z_recv,
    e_send,
    e_recv,
):
    n_tm, n_space, steps, rows, cells, samples, own, chunks = dims
    per = own // chunks
    total = 2 * NL * BW
    tm, space, span = lax.axis_index("tm"), lax.axis_index("space"), lax.axis_index("span")
    group = n_space * per
    tiles = cells // LANES
    pitch = tiles * rows
    flat = fields.reshape(total * pitch, LANES)

    def peer_tm(d):
        return {"tm": lax.rem(tm + d, n_tm)}

    def peer_space(d):
        return {"space": lax.rem(space + d, n_space)}

    other = {"span": 1 - span}

    barrier = pltpu.get_barrier_semaphore()
    for d in range(1, n_tm):
        pl.semaphore_signal(barrier, inc=1, device_id=peer_tm(d), device_id_type=MESH)
    for d in range(1, n_space):
        pl.semaphore_signal(barrier, inc=1, device_id=peer_space(d), device_id_type=MESH)
    pl.semaphore_signal(barrier, inc=1, device_id=other, device_id_type=MESH)

    packed[tm] = small_ref[0:8]
    square = (rows, rows)
    diagonal = lax.broadcasted_iota(jnp.int32, square, 0) == lax.broadcasted_iota(
        jnp.int32, square, 1
    )
    column = jnp.sum(
        jnp.where(diagonal, jnp.broadcast_to(small_ref[8:9, 0:rows], square), 0.0), axis=1, keepdims=True
    )
    mine = pl.ds(pl.multiple_of(space * rows, 8), rows)
    metrics[mine, :] = jnp.broadcast_to(0.5 * column, (rows, LANES))

    def split(r, carry):
        from_row = lax.div(r, 8) * (8 * tiles) + lax.rem(r, 8)
        value = jnp.concatenate(
            [x_ref[pl.ds(from_row + 8 * v, steps, stride=pitch), :] for v in range(tiles)], axis=1
        )
        high, middle, low = three(value)
        for k, part in enumerate((high, middle, low, high, middle, high)):
            parts[r, k * steps : (k + 1) * steps, :] = part.astype(jnp.bfloat16)
        return carry

    lax.fori_loop(0, rows, split, 0, unroll=2)

    pl.semaphore_wait(barrier, n_tm - 1 + n_space - 1 + 1)

    started = []
    pk_copies = []
    for d in range(1, n_tm):
        copy = pltpu.make_async_remote_copy(
            packed.at[tm], packed.at[tm], pk_send.at[d - 1], pk_recv.at[d - 1],
            device_id=peer_tm(d), device_id_type=MESH,
        )
        copy.start()
        pk_copies.append(copy)
    mt_copies = []
    for d in range(1, n_space):
        copy = pltpu.make_async_remote_copy(
            metrics.at[mine, :], metrics.at[mine, :], mt_send.at[d - 1], mt_recv.at[d - 1],
            device_id=peer_space(d), device_id_type=MESH,
        )
        copy.start()
        mt_copies.append(copy)

    for g in range(own):
        for v in range(tiles):
            final[g, v, 0:PAD, :] = jnp.zeros((PAD, LANES), jnp.float32)
            final[g, v, PAD + n_space * rows :, :] = jnp.zeros((PAD, LANES), jnp.float32)

    p = lax.broadcasted_iota(jnp.int32, (total, LANES), 0)
    lane = lax.broadcasted_iota(jnp.int32, (total, LANES), 1)
    low = lax.rem(p, per)
    i = lax.rem(lax.div(p, per), n_space)
    j = lax.rem(lax.div(p, per * n_space), n_tm)
    c = lax.div(p, per * n_space * n_tm)
    g = (i * n_tm + j) * own + c * per + low
    listed = g >> 1
    band_pos = lax.div(listed, BW)
    bands = small_ref[9:10].astype(jnp.int32)
    band = jnp.zeros_like(p)
    for b in range(NL):
        band = jnp.where(band_pos == b, bands[:, b : b + 1], band)
    frequency = band * BW + lax.rem(listed, BW)
    quarter = (NT // 4) * (g & 1)

    def dft(q):
        t = q * samples + lane
        phase = (frequency * t + quarter) & (NT - 1)
        window = 0.5 - 0.5 * cosine(t & (NT - 1))
        return cosine(phase) * (window / math.sqrt(NT))

    waves = [dft(lax.rem(tm + n_tm - d, n_tm)) for d in range(n_tm)]

    step = tm * steps + lax.broadcasted_iota(jnp.int32, (steps, LANES), 0)
    mixed = None
    for d in range(n_tm):
        q = lax.rem(tm + n_tm - d, n_tm)
        if d > 0:
            pk_copies[d - 1].wait_recv()
        table = packed[q]
        slot = step - table[6:7].astype(jnp.int32)
        slot = jnp.where(slot < table[7:8].astype(jnp.int32), slot, -1)
        weights = jnp.zeros((steps, LANES), jnp.float32)
        for s in range(SLOTS):
            weights = jnp.where(slot == s, table[s : s + 1], weights)
        term = lax.dot_general(
            waves[d], jnp.concatenate([weights] * 6, axis=0), (((1,), (1,)), ((), ())),
            precision=HIGHEST, preferred_element_type=jnp.float32,
        )
        mixed = term if mixed is None else mixed + term
    high, middle, low = three(mixed)
    at = lax.broadcasted_iota(jnp.int32, mixed.shape, 1)
    mixing[...] = jnp.where(
        at < 3 * steps, high, jnp.where(at < 5 * steps, middle, low)
    ).astype(jnp.bfloat16)

    rows_per = n_tm * group
    x_copies, z_copies, e_copies = {}, {}, {}

    def start_x(c):
        left = mixing[c * rows_per : (c + 1) * rows_per, :]

        def body(r, carry):
            value = jnp.dot(left, parts[r], preferred_element_type=jnp.float32)
            for v in range(tiles):
                flat[pl.ds(c * rows_per * pitch + v * rows + r, rows_per, stride=pitch), :] = value[
                    :, v * LANES : (v + 1) * LANES
                ]
            return carry

        lax.fori_loop(0, rows, body, 0, unroll=4)
        x_copies[c] = []
        for d in range(1, n_tm):
            to = lax.rem(tm + d, n_tm)
            copy = pltpu.make_async_remote_copy(
                fields.at[pl.ds((c * n_tm + to) * group, group)],
                arrived.at[c, d - 1],
                x_send.at[c, d - 1], x_recv.at[c, d - 1],
                device_id=peer_tm(d), device_id_type=MESH,
            )
            copy.start()
            x_copies[c].append(copy)

    def start_z(c):
        for copy in x_copies[c]:
            copy.wait_recv()
        base = (c * n_tm + tm) * group

        def body(k, carry):
            value = fields[base + k]
            for d in range(1, n_tm):
                value = value + arrived[c, d - 1, k]
            fields[base + k] = value
            return carry

        lax.fori_loop(0, group, body, 0, unroll=min(4, group))
        z_copies[c] = []
        there = pl.ds(pl.multiple_of(PAD + space * rows, 8), rows)
        for d in range(1, n_space):
            to = lax.rem(space + d, n_space)
            copy = pltpu.make_async_remote_copy(
                fields.at[pl.ds(base + to * per, per)],
                final.at[pl.ds(c * per, per), pl.ds(0, tiles), there, :],
                z_send.at[c, d - 1], z_recv.at[c, d - 1],
                device_id=peer_space(d), device_id_type=MESH,
            )
            copy.start()
            z_copies[c].append(copy)
        for k in range(per):
            final[c * per + k, 0:tiles, there, :] = fields[base + space * per + k]

    inner = pl.ds(PAD, n_space * rows)

    def start_e(c):
        for copy in z_copies[c]:
            copy.wait_recv()
        first = lax.broadcasted_iota(jnp.int32, (n_space * rows, LANES), 1) == 0
        for k in range(per):
            g = c * per + k
            edges[g] = jnp.where(
                first, final[g, 0, inner, :], final[g, tiles - 1, inner, :]
            )
        copy = pltpu.make_async_remote_copy(
            edges.at[pl.ds(c * per, per)],
            final.at[pl.ds(c * per, per), tiles, inner, :],
            e_send.at[c], e_recv.at[c],
            device_id=other, device_id_type=MESH,
        )
        copy.start()
        e_copies[c] = copy

    def finish(c):
        e_copies[c].wait_recv()
        scale = metrics[...]
        for k in range(per):
            g = c * per + k
            for v in range(tiles):
                above = final[g, v, PAD + 1 : PAD + 1 + n_space * rows, :]
                below = final[g, v, PAD - 1 : PAD - 1 + n_space * rows, :]
                out_ref[g, 0, :, v * LANES : (v + 1) * LANES] = scale * (above - below)
            ring = jnp.concatenate([final[g, v, inner, :] for v in range(tiles + 1)], axis=1)
            after = pltpu.roll(ring, cells + LANES - 1, 1)
            before = pltpu.roll(ring, 1, 1)
            out_ref[g, 1] = 0.5 * (after - before)[:, 0:cells]

    for c in range(min(AHEAD, chunks)):
        start_x(c)
    for s in range(chunks + Z_LAG + E_LAG):
        if s < chunks:
            start_z(s)
        if s + AHEAD < chunks:
            start_x(s + AHEAD)
        if s == 1:
            for copy in mt_copies:
                copy.wait_recv()
        if 0 <= s - Z_LAG < chunks:
            start_e(s - Z_LAG)
        if 0 <= s - Z_LAG - E_LAG < chunks:
            finish(s - Z_LAG - E_LAG)

    for copy in pk_copies + mt_copies:
        copy.wait_send()
    for c in range(chunks):
        for copy in x_copies[c] + z_copies[c] + [e_copies[c]]:
            copy.wait_send()


def shards(snapshots, lagrange_weights, source_start, band_len, band_list, row_metric):
    n_tm, n_space = lax.axis_size("tm"), lax.axis_size("space")
    steps, rows, cells = snapshots.shape
    samples = source_start.shape[0]
    total = 2 * NL * BW
    own = total // (n_tm * n_space)
    chunks = math.gcd(own, CHUNKS)
    per = own // chunks
    f32 = jnp.float32
    dims = (n_tm, n_space, steps, rows, cells, samples, own, chunks)

    def line(value):
        row = value.astype(f32).reshape(-1, value.shape[-1])
        return jnp.pad(row, ((0, 0), (0, LANES - row.shape[1])))

    small = jnp.concatenate(
        [line(v) for v in (lagrange_weights.T, source_start, band_len, row_metric, band_list)]
        + [jnp.zeros((6, LANES), f32)]
    )
    vmem = pl.BlockSpec(memory_space=pltpu.VMEM)
    dma = pltpu.SemaphoreType.DMA
    return pl.pallas_call(
        functools.partial(kernel, dims),
        out_shape=jax.ShapeDtypeStruct((own, 2, n_space * rows, cells), f32),
        in_specs=[vmem, vmem],
        out_specs=vmem,
        scratch_shapes=[
            pltpu.VMEM((rows, 6 * steps, cells), jnp.bfloat16),
            pltpu.VMEM((n_tm, 8, LANES), f32),
            pltpu.VMEM((n_space * rows, LANES), f32),
            pltpu.VMEM((total, 6 * steps), jnp.bfloat16),
            pltpu.VMEM((total, cells // LANES, rows, LANES), f32),
            pltpu.VMEM((chunks, n_tm - 1, n_space * per, cells // LANES, rows, LANES), f32),
            pltpu.VMEM((own, cells // LANES + 1, n_space * rows + 2 * PAD, LANES), f32),
            pltpu.VMEM((own, n_space * rows, LANES), f32),
            dma((n_tm - 1,)),
            dma((n_tm - 1,)),
            dma((n_space - 1,)),
            dma((n_space - 1,)),
            dma((chunks, n_tm - 1)),
            dma((chunks, n_tm - 1)),
            dma((chunks, n_space - 1)),
            dma((chunks, n_space - 1)),
            dma((chunks,)),
            dma((chunks,)),
        ],
        compiler_params=pltpu.CompilerParams(
            collective_id=0, has_side_effects=True, vmem_limit_bytes=32 * 1024 * 1024
        ),
    )(
        snapshots.reshape(steps, rows // 8, 8, cells // LANES, LANES)
        .swapaxes(2, 3)
        .reshape(steps * rows * (cells // LANES), LANES),
        small,
    )


def solution(mesh):
    placed = (
        P(("blocks", "tm"), "space", "span"),
        P(("blocks", "tm"), None),
        P(("blocks", "tm")),
        P(("blocks", "tm")),
        P(),
        P("space"),
    )
    return jax.shard_map(
        shards,
        mesh=mesh,
        in_specs=placed,
        out_specs=P(("blocks", "space", "tm"), None, None, "span"),
        check_vma=False,
    )
```
